32 devices in a mesh: row: 4 (over y, x), col: 8 (over z, core).
Axes of the slice: x: 2, y: 2, z: 4, core: 2. Of those that a mesh axis runs over, the one named last changes fastest.
Arguments:
- object_field: float32 [2, 2048, 4096], P(None, 'row', 'col'), may hold values from -5 to 5
- probe: float32 [2, 8, 256, 256], replicated, may hold values from -2.5 to 2.5
- intensity: float32 [64, 256, 256], P(('row', 'col')), may hold values from 0.5 to 4
- row_offset: int32 [64], P(('row', 'col')), may hold values from 0 to 511
- col_offset: int32 [64], P(('row', 'col')), may hold values from 0 to 511
- live: int32 [64], P(('row', 'col')), may hold values 0 or 1
Outputs:
- object_grad: float32 [2, 2048, 4096], P(None, 'row', 'col')
- probe_grad: float32 [2, 8, 256, 256], replicated
The draws below stay inside these ranges and needn't reach their ends.
All inputs are finite; a program needn't handle non-finite values. No bound on the sum of `live` on one device may be relied on, other than what follows from the above.
Results may differ from the reference program's by a relative error of at most 0.0003.
Values sent between devices are 32-bit elements; how exact they have to be, the bound alone decides.
No kernel may reach another device: no remote copies, remote signals or barrier semaphores. Data moves between devices by JAX's collectives and lax.ppermute only.
A program may use at most 128 MiB of HBM per device.

```python
import jax
import jax.numpy as jnp
from jax import lax

W = 256
MODES = 8
TR = 512
TC = 512
NR = 2048
NC = 4096
NPAT = 64
N_ROW = 4
N_COL = 8


def touch_ends(result, key, low, high):
    shape = result.shape
    place = [jax.random.randint(jax.random.fold_in(key, axis), (), 0, shape[axis]) for axis in range(len(shape))]
    result = result.at[tuple(place)].set(low)
    longest = shape.index(max(shape))
    place[longest] = (place[longest] + 1) % shape[longest]
    return result.at[tuple(place)].set(high)


def steps_of(stream_key, dims, pieces, least, high):
    def one(position, blocks):
        heights = jax.random.uniform(jax.random.fold_in(jax.random.fold_in(stream_key, 6), position), (blocks,), jnp.float32, least / len(pieces), high / len(pieces))
        return jnp.repeat(jnp.exp(heights), dims[position] // blocks).reshape((-1,) + (1,) * (len(dims) - position - 1))

    loudness = one(*pieces[0])
    for cut in pieces[1:]:
        loudness = loudness * one(*cut)
    return loudness


def bell_draw(own_key, shape, scale, limit, pieces=(), kind=jnp.bfloat16):
    values = jax.random.normal(own_key, shape, jnp.float32) * scale
    if len(pieces) > 0:
        values = steps_of(own_key, shape, pieces, -0.22, 0.18) * values
    return jnp.clip(values, min=-limit, max=limit).astype(kind)


def setup_inputs(seed: int = 0) -> dict:
    streams_of = jax.random.split(jax.random.key(seed), 7)
    return {
        "object_field": bell_draw(streams_of[0], (2, NR, NC), 0.7, 5.0, ((1, 4), (2, 8)), jnp.float32),
        "probe": bell_draw(streams_of[1], (2, MODES, W, W), 0.35, 2.5, (), jnp.float32),
        "intensity": jnp.clip(0.5 + 3.5 * jax.random.uniform(streams_of[2], (NPAT, W, W), jnp.float32) ** steps_of(streams_of[2], (NPAT, W, W), ((0, 32),), -0.2, 0.2), 0.5, 4.0),
        "row_offset": touch_ends(jax.random.randint(streams_of[3], (NPAT,), 0, TR), jax.random.fold_in(streams_of[3], 1), 0, TR - 1).astype(jnp.int32),
        "col_offset": touch_ends(jax.random.randint(streams_of[4], (NPAT,), 0, TC), jax.random.fold_in(streams_of[4], 1), 0, TC - 1).astype(jnp.int32),
        "live": touch_ends((jax.random.randint(streams_of[5], (NPAT,), 0, 4) < 3).astype(jnp.int32), jax.random.fold_in(streams_of[5], 1), 0, 1),
    }


smoothing = 0.25

def reference(object_field, probe, intensity, row_offset, col_offset, live):
    width = probe.shape[-1]
    total_rows = object_field.shape[1]
    total_cols = object_field.shape[2]
    per_device = intensity.shape[0] // (N_ROW * N_COL)
    padded = jnp.pad(object_field, ((0, 0), (0, width), (0, width)))
    probe_re = probe[0]
    probe_im = probe[1]
    live_float = live.astype(jnp.float32)

    def one_pattern(carry, index):
        grad_object, grad_probe = carry
        block = index // per_device
        top = (block // N_COL * TR + row_offset[index]).astype(jnp.int32)
        left = (block % N_COL * TC + col_offset[index]).astype(jnp.int32)
        anchor = jnp.zeros((), jnp.int32)
        patch = lax.dynamic_slice(padded, (anchor, top, left), (2, width, width))
        patch_re = patch[0][None]
        patch_im = patch[1][None]
        exit_re = probe_re * patch_re - probe_im * patch_im
        exit_im = probe_re * patch_im + probe_im * patch_re
        spectrum = jnp.fft.fft2(lax.complex(exit_re, exit_im), norm='ortho')
        spec_re = jnp.real(spectrum)
        spec_im = jnp.imag(spectrum)
        amplitude = jnp.sqrt(lax.optimization_barrier(jnp.sum(spec_re * spec_re + spec_im * spec_im, axis=0)) + smoothing)
        factor = (1.0 - jnp.sqrt(intensity[index]) / amplitude) * live_float[index]
        back = jnp.fft.ifft2(lax.complex(spec_re * factor, spec_im * factor), norm='ortho')
        chi_re = jnp.real(back)
        chi_im = jnp.imag(back)
        obj_re = lax.optimization_barrier(jnp.sum(probe_re * chi_re + probe_im * chi_im, axis=0))
        obj_im = lax.optimization_barrier(jnp.sum(probe_re * chi_im - probe_im * chi_re, axis=0))
        contrib = jnp.stack([obj_re, obj_im])
        current = lax.dynamic_slice(grad_object, (anchor, top, left), (2, width, width))
        grad_object = lax.dynamic_update_slice(grad_object, current + contrib, (anchor, top, left))
        pro_re = patch_re * chi_re + patch_im * chi_im
        pro_im = patch_re * chi_im - patch_im * chi_re
        grad_probe = grad_probe + jnp.stack([pro_re, pro_im])
        return ((grad_object, grad_probe), None)
    start = (jnp.zeros_like(padded), jnp.zeros_like(probe))
    indices = jnp.arange(intensity.shape[0], dtype=jnp.int32)
    (grad_object, grad_probe), _ = lax.scan(one_pattern, start, indices)
    return (grad_object[:, :total_rows, :total_cols], grad_probe)
```

```python
import functools

import jax
import jax.numpy as jnp
import ml_dtypes
import numpy as np
from jax import lax
from jax.experimental import pallas as pl
from jax.experimental.pallas import tpu as pltpu
from jax.sharding import PartitionSpec as P

smoothing = 0.25


def passed_along(array, axis, by):
    devices = lax.axis_size(axis)
    pairs = [(i, i + by) for i in range(devices) if 0 <= i + by < devices]
    return lax.ppermute(array, axis, pairs)


def split(x):
    high = x.astype(jnp.bfloat16)
    return high, (x - high.astype(jnp.float32)).astype(jnp.bfloat16)


def matrices(width):
    half = width // 2
    n = np.arange(half)
    scale = 1.0 / np.sqrt(width)
    out = []
    forward_right, forward_left, inverse_left, inverse_right = [], [], [], []
    for parity in (0, 1):
        phase = (n[:, None] * (2 * n[None, :] + parity) % width) * (2.0 * np.pi / width)
        c, s = np.cos(phase) * scale, np.sin(phase) * scale
        forward_right.append(np.block([[c, -s], [s, c]]))
        forward_left.append(np.block([[c.T, s.T], [-s.T, c.T]]))
        inverse_left.append(np.block([[c, -s], [s, c]]))
        inverse_right.append(np.block([[c.T, s.T], [-s.T, c.T]]))
    for pair in (forward_right, forward_left, inverse_left, inverse_right):
        for m in pair:
            high = m.astype(np.float32).astype(ml_dtypes.bfloat16)
            low = (m - high.astype(np.float64)).astype(np.float32).astype(ml_dtypes.bfloat16)
            out += [high, low]
    return np.stack(out)


def dot(a, b):
    return jnp.dot(a, b, preferred_element_type=jnp.float32)


def right(z, mats, at):
    high, low = split(z)
    return dot(high, mats[at]) + (dot(low, mats[at]) + dot(high, mats[at + 1]))


def left(z, mats, at):
    high, low = split(z)
    return dot(mats[at], high) + (dot(mats[at], low) + dot(mats[at + 1], high))


def kernel(
    row_ref, col_ref, live_ref, bit_ref, own, beside, below0, below1, corner, probe, root, mats,
    g_own, g_beside, g_below, g_corner, p_keep, p_send,
    ext, grad, spec, patch, factor, placed, sems,
):
    patterns, width = root.shape[0], root.shape[-1]
    modes = probe.shape[1]
    half = width // 2
    rows, cols = own.shape[1], own.shape[2]
    keep = modes // 2

    def part(e, top, height, left_of, wide):
        return e.at[:, pl.ds(top, height), pl.ds(left_of, wide)]

    arriving = [
        pltpu.make_async_copy(src, dst, sems.at[i])
        for i, (src, dst) in enumerate(
            (
                (own, part(ext, 0, rows, 0, cols)),
                (beside, part(ext, 0, rows, cols, width)),
                (below0, part(ext, rows, width, 0, width)),
                (below1, part(ext, rows, width, width, cols - width)),
                (corner, part(ext, rows, width, cols, width)),
            )
        )
    ]
    for copy in arriving:
        copy.start()
    grad[...] = jnp.zeros_like(grad)
    for copy in arriving:
        copy.wait()

    tall, wide = width + 8, width + 128

    def turned(x, by, axis):
        return pltpu.roll(x, jnp.where(by == 0, 0, x.shape[axis] - by), axis)

    for p in range(patterns):
        top = pl.multiple_of((row_ref[p] // 8) * 8, 8)
        drop = row_ref[p] % 8
        base = pl.multiple_of((col_ref[p] // 128) * 128, 128)
        shift = col_ref[p] % 128
        for c in range(2):
            window = turned(ext[c, pl.ds(top, tall), pl.ds(base, wide)], drop, 0)[:width]
            patch[c] = turned(window, shift, 1)[:, :width]
        factor[...] = jnp.zeros_like(factor)

        def forward(m, carry):
            o_re, o_im = patch[0], patch[1]
            q_re, q_im = probe[0, m], probe[1, m]
            e_re = q_re * o_re - q_im * o_im
            e_im = q_re * o_im + q_im * o_re
            r0, r1 = e_re[:, :half], e_re[:, half:]
            i0, i1 = e_im[:, :half], e_im[:, half:]
            even = right(jnp.concatenate([r0 + r1, i0 + i1], axis=1), mats, 0)
            odd = right(jnp.concatenate([r0 - r1, i0 - i1], axis=1), mats, 2)
            re = jnp.concatenate([even[:, :half], odd[:, :half]], axis=1)
            im = jnp.concatenate([even[:, half:], odd[:, half:]], axis=1)
            f0 = left(jnp.concatenate([re[:half] + re[half:], im[:half] + im[half:]], axis=0), mats, 4)
            f1 = left(jnp.concatenate([re[:half] - re[half:], im[:half] - im[half:]], axis=0), mats, 6)
            spec[m, 0] = f0
            spec[m, 1] = f1
            factor[0] += f0[:half] * f0[:half] + f0[half:] * f0[half:]
            factor[1] += f1[:half] * f1[:half] + f1[half:] * f1[half:]
            return carry

        lax.fori_loop(0, modes, forward, 0)
        alive = live_ref[p].astype(jnp.float32)
        factor[...] = (1.0 - root[p] / jnp.sqrt(factor[...] + smoothing)) * alive
        placed[...] = jnp.zeros_like(placed)

        def backward(out, first, j, carry):
            group = (j // (modes // 4)) % 2
            m = j ^ bit_ref[0] ^ bit_ref[1 + group]
            scale0 = factor[0]
            scale1 = factor[1]
            e = left(spec[m, 0] * jnp.concatenate([scale0, scale0], axis=0), mats, 8)
            o = left(spec[m, 1] * jnp.concatenate([scale1, scale1], axis=0), mats, 10)
            total, other = e + o, e - o
            re = jnp.concatenate([total[:half], other[:half]], axis=0)
            im = jnp.concatenate([total[half:], other[half:]], axis=0)
            even = right(jnp.concatenate([re[:, :half], im[:, :half]], axis=1), mats, 12)
            odd = right(jnp.concatenate([re[:, half:], im[:, half:]], axis=1), mats, 14)
            total, other = even + odd, even - odd
            x_re = jnp.concatenate([total[:, :half], other[:, :half]], axis=1)
            x_im = jnp.concatenate([total[:, half:], other[:, half:]], axis=1)
            q_re, q_im = probe[0, m], probe[1, m]
            placed[0, :width, :width] += q_re * x_re + q_im * x_im
            placed[1, :width, :width] += q_re * x_im - q_im * x_re
            o_re, o_im = patch[0], patch[1]
            gains = (o_re * x_re + o_im * x_im, o_re * x_im - o_im * x_re)
            for c in range(2):
                for h in range(2):
                    down = pl.multiple_of((h ^ bit_ref[5]) * half, half)
                    at = (j - first, c ^ bit_ref[3 + group], pl.ds(down, half))
                    value = gains[c][h * half : (h + 1) * half]
                    if p == 0:
                        out[at] = value
                    else:
                        out[at] = out[at] + value
            return carry

        lax.fori_loop(keep, modes, functools.partial(backward, p_send, keep), 0)
        lax.fori_loop(0, keep, functools.partial(backward, p_keep, 0), 0)
        for c in range(2):
            at = (c, pl.ds(top, tall), pl.ds(base, wide))
            grad[at] = grad[at] + pltpu.roll(pltpu.roll(placed[c], drop, 0), shift, 1)

    leaving = [
        pltpu.make_async_copy(src, dst, sems.at[i])
        for i, (src, dst) in enumerate(
            (
                (part(grad, 0, rows, 0, cols), g_own),
                (part(grad, 0, rows, cols, width), g_beside),
                (part(grad, rows, width, 0, cols), g_below),
                (part(grad, rows, width, cols, width), g_corner),
            )
        )
    ]
    for copy in leaving:
        copy.start()
    for copy in leaving:
        copy.wait()


def parity_order(intensity, orders, root):
    half = root.shape[2]

    def parts(x):
        high, low = split(x)
        return high, low, (x - high.astype(jnp.float32) - low.astype(jnp.float32)).astype(jnp.bfloat16)

    for p in range(root.shape[0]):
        high, middle, low = parts(jnp.sqrt(intensity[p]))
        x = dot(orders[0], high) + dot(orders[0], middle) + dot(orders[0], low)
        high, middle, low = parts(x)
        x = dot(high, orders[1]) + dot(middle, orders[1]) + dot(low, orders[1])
        root[p, 0] = x[:half]
        root[p, 1] = x[half:]


def assemble(bit_ref, *refs):
    pieces, out, sems = refs[:-2], refs[-2], refs[-1]
    modes, width = out.shape[1], out.shape[-1]
    half = width // 2
    each = modes // len(pieces)
    copies = []
    for slot in range(modes):
        piece, inner = divmod(slot, each)
        group = (slot // (modes // 4)) % 2
        m = slot ^ bit_ref[0] ^ bit_ref[1 + group]
        for c in range(2):
            for h in range(2):
                down = pl.multiple_of((h ^ bit_ref[5]) * half, half)
                copies.append(
                    pltpu.make_async_copy(
                        pieces[piece].at[inner, c, pl.ds(h * half, half)],
                        out.at[c ^ bit_ref[3 + group], m, pl.ds(down, half)],
                        sems.at[len(copies)],
                    )
                )
    for copy in copies:
        copy.start()
    for copy in copies:
        copy.wait()


def swap(array, where):
    axis, bit = where
    return lax.ppermute(array, axis, [(i, i ^ (1 << bit)) for i in range(lax.axis_size(axis))])


def bit_of(where):
    axis, bit = where
    return (lax.axis_index(axis) >> bit) & 1


def probe_sum(p_keep, p_send, bits, order):
    core, first, second, third, rest = order
    keep, width = p_keep.shape[0], p_keep.shape[-1]
    one = keep // 4
    half = width // 2
    came = swap(p_send, core)
    a_came = swap(p_keep[one : 2 * one] + came[one : 2 * one], first)
    b_came = swap(p_keep[3 * one :] + came[3 * one :], second)

    def a_of(at):
        return p_keep[:one, at] + came[:one, at] + a_came[:, at]

    def b_of(at):
        return p_keep[2 * one : 3 * one, at] + came[2 * one : 3 * one, at] + b_came[:, at]

    a_more = swap(a_of(1), second)
    b_more = swap(b_of(1), first)
    both = jnp.stack([a_of(0) + a_more, b_of(0) + b_more])
    z_came = swap(both[:, :, half:], third)
    z = both[:, :, :half] + z_came
    for where in rest:
        z = z + swap(z, where)
    z_other = swap(z, third)
    a = jnp.concatenate([z[0], z_other[0]], axis=1)
    b = jnp.concatenate([z[1], z_other[1]], axis=1)
    a = jnp.stack([a, swap(a, second)], axis=1)
    b = jnp.stack([b, swap(b, first)], axis=1)
    pieces = [a, swap(a, first), b, swap(b, second)]
    pieces = pieces + [swap(piece, core) for piece in pieces]
    modes = 2 * keep
    return pl.pallas_call(
        assemble,
        out_shape=jax.ShapeDtypeStruct((2, modes, width, width), jnp.float32),
        in_specs=[pl.BlockSpec(memory_space=pltpu.SMEM)] + [pl.BlockSpec(memory_space=pltpu.VMEM)] * len(pieces),
        out_specs=pl.BlockSpec(memory_space=pl.ANY),
        scratch_shapes=[pltpu.SemaphoreType.DMA((4 * modes,))],
        compiler_params=pltpu.CompilerParams(vmem_limit_bytes=24 * 1024 * 1024),
    )(bits, *pieces)


def shards(object_field, probe, intensity, row_offset, col_offset, live):
    width = probe.shape[-1]
    modes = probe.shape[1]
    patterns = intensity.shape[0]
    half = width // 2
    rows, cols = object_field.shape[1:]
    row_bits = [("row", i) for i in range(lax.axis_size("row").bit_length() - 1)]
    col_bits = [("col", i) for i in range(lax.axis_size("col").bit_length() - 1)]
    core, first, second = col_bits[0], row_bits[0], row_bits[1]
    others = col_bits[1:] + row_bits[2:]
    order = (core, first, second, others[0], others[1:])

    below0 = passed_along(object_field[:, :width, :width], "row", -1)
    below1 = passed_along(object_field[:, :width, width:], "row", -1)
    beside = passed_along(object_field[:, :, :width], "col", -1)
    corner = passed_along(below0, "col", -1)
    smem = pl.BlockSpec(memory_space=pltpu.SMEM)
    vmem = pl.BlockSpec(memory_space=pltpu.VMEM)
    hbm = pl.BlockSpec(memory_space=pl.ANY)
    f32 = jnp.float32
    order_rows = np.eye(width)[np.concatenate([np.arange(0, width, 2), np.arange(1, width, 2)])]
    root = pl.pallas_call(
        parity_order,
        out_shape=jax.ShapeDtypeStruct((patterns, 2, half, width), f32),
        in_specs=[vmem, vmem],
        out_specs=vmem,
    )(intensity, jnp.asarray(np.stack([order_rows, order_rows.T]), jnp.bfloat16))
    bits = jnp.stack(
        [
            bit_of(core) * (modes // 2),
            bit_of(first) * (modes // 8),
            bit_of(second) * (modes // 8),
            bit_of(second),
            bit_of(first),
            bit_of(others[0]),
        ]
    ).astype(jnp.int32)
    mats = jnp.asarray(matrices(width))
    g_own, g_beside, g_below, g_corner, p_keep, p_send = pl.pallas_call(
        kernel,
        out_shape=(
            jax.ShapeDtypeStruct((2, rows, cols), f32),
            jax.ShapeDtypeStruct((2, rows, width), f32),
            jax.ShapeDtypeStruct((2, width, cols), f32),
            jax.ShapeDtypeStruct((2, width, width), f32),
            jax.ShapeDtypeStruct((modes // 2, 2, width, width), f32),
            jax.ShapeDtypeStruct((modes // 2, 2, width, width), f32),
        ),
        in_specs=[smem] * 4 + [hbm] * 5 + [vmem] * 3,
        out_specs=(hbm, hbm, hbm, hbm, vmem, vmem),
        scratch_shapes=[
            pltpu.VMEM((2, rows + width, cols + width), f32),
            pltpu.VMEM((2, rows + width, cols + width), f32),
            pltpu.VMEM((modes, 2, width, width), f32),
            pltpu.VMEM((2, width, width), f32),
            pltpu.VMEM((2, half, width), f32),
            pltpu.VMEM((2, width + 8, width + 128), f32),
            pltpu.SemaphoreType.DMA((5,)),
        ],
        compiler_params=pltpu.CompilerParams(vmem_limit_bytes=48 * 1024 * 1024),
    )(row_offset, col_offset, live, bits, object_field, beside, below0, below1, corner, probe, root, mats)

    probe_grad = probe_sum(p_keep, p_send, bits, order)
    below_grad = g_below.at[:, :, :width].add(passed_along(g_corner, "col", 1))
    from_left = passed_along(g_beside, "col", 1)
    from_above = passed_along(below_grad, "row", 1)
    object_grad = g_own.at[:, :, :width].add(from_left)
    object_grad = object_grad.at[:, :width, :].add(from_above)
    return (object_grad, probe_grad)


def solution(mesh):
    in_specs = (
        P(None, "row", "col"),
        P(),
        P(("row", "col"), None, None),
        P(("row", "col")),
        P(("row", "col")),
        P(("row", "col")),
    )
    out_specs = (P(None, "row", "col"), P())
    return jax.shard_map(shards, mesh=mesh, in_specs=in_specs, out_specs=out_specs, check_vma=False)
```

```python
import functools

import jax
import jax.numpy as jnp
import ml_dtypes
import numpy as np
from jax import lax
from jax.experimental import pallas as pl
from jax.experimental.pallas import tpu as pltpu
from jax.sharding import PartitionSpec as P

smoothing = 0.25


def passed_along(array, axis, by):
    devices = lax.axis_size(axis)
    pairs = [(i, i + by) for i in range(devices) if 0 <= i + by < devices]
    return lax.ppermute(array, axis, pairs)


def split(x):
    high = x.astype(jnp.bfloat16)
    return high, (x - high.astype(jnp.float32)).astype(jnp.bfloat16)


def matrices(width):
    half = width // 2
    n = np.arange(half)
    scale = 1.0 / np.sqrt(width)
    out = []
    forward_right, forward_left, inverse_left, inverse_right = [], [], [], []
    for parity in (0, 1):
        phase = (n[:, None] * (2 * n[None, :] + parity) % width) * (2.0 * np.pi / width)
        c, s = np.cos(phase) * scale, np.sin(phase) * scale
        forward_right.append(np.block([[c, -s], [s, c]]))
        forward_left.append(np.block([[c.T, s.T], [-s.T, c.T]]))
        inverse_left.append(np.block([[c, -s], [s, c]]))
        inverse_right.append(np.block([[c.T, s.T], [-s.T, c.T]]))
    for pair in (forward_right, forward_left, inverse_left, inverse_right):
        for m in pair:
            high = m.astype(np.float32).astype(ml_dtypes.bfloat16)
            low = (m - high.astype(np.float64)).astype(np.float32).astype(ml_dtypes.bfloat16)
            out += [high, low]
    return np.stack(out)


def dot(a, b):
    return jnp.dot(a, b, preferred_element_type=jnp.float32)


def right(z, mats, at):
    high, low = split(z)
    return dot(high, mats[at]) + (dot(low, mats[at]) + dot(high, mats[at + 1]))


def left(z, mats, at):
    high, low = split(z)
    return dot(mats[at], high) + (dot(mats[at], low) + dot(mats[at + 1], high))


def kernel(
    row_ref, col_ref, live_ref, bit_ref, own, beside, below0, below1, corner, probe, root, mats,
    g_own, g_beside, g_below, g_corner, keep0, keep1, send0, send1,
    ext, grad, spec, patch, factor, placed, sems,
):
    patterns, width = root.shape[0], root.shape[-1]
    modes = probe.shape[1]
    half = width // 2
    rows, cols = own.shape[1], own.shape[2]
    keep = modes // 2

    def part(e, top, height, left_of, wide):
        return e.at[:, pl.ds(top, height), pl.ds(left_of, wide)]

    arriving = [
        pltpu.make_async_copy(src, dst, sems.at[i])
        for i, (src, dst) in enumerate(
            (
                (own, part(ext, 0, rows, 0, cols)),
                (beside, part(ext, 0, rows, cols, width)),
                (below0, part(ext, rows, width, 0, width)),
                (below1, part(ext, rows, width, width, cols - width)),
                (corner, part(ext, rows, width, cols, width)),
            )
        )
    ]
    for copy in arriving:
        copy.start()
    grad[...] = jnp.zeros_like(grad)
    for copy in arriving:
        copy.wait()

    tall, wide = width + 8, width + 128

    def turned(x, by, axis):
        return pltpu.roll(x, jnp.where(by == 0, 0, x.shape[axis] - by), axis)

    for p in range(patterns):
        top = pl.multiple_of((row_ref[p] // 8) * 8, 8)
        drop = row_ref[p] % 8
        base = pl.multiple_of((col_ref[p] // 128) * 128, 128)
        shift = col_ref[p] % 128
        for c in range(2):
            window = turned(ext[c, pl.ds(top, tall), pl.ds(base, wide)], drop, 0)[:width]
            patch[c] = turned(window, shift, 1)[:, :width]
        factor[...] = jnp.zeros_like(factor)

        def forward(m, carry):
            o_re, o_im = patch[0], patch[1]
            q_re, q_im = probe[0, m], probe[1, m]
            e_re = q_re * o_re - q_im * o_im
            e_im = q_re * o_im + q_im * o_re
            r0, r1 = e_re[:, :half], e_re[:, half:]
            i0, i1 = e_im[:, :half], e_im[:, half:]
            even = right(jnp.concatenate([r0 + r1, i0 + i1], axis=1), mats, 0)
            odd = right(jnp.concatenate([r0 - r1, i0 - i1], axis=1), mats, 2)
            re = jnp.concatenate([even[:, :half], odd[:, :half]], axis=1)
            im = jnp.concatenate([even[:, half:], odd[:, half:]], axis=1)
            f0 = left(jnp.concatenate([re[:half] + re[half:], im[:half] + im[half:]], axis=0), mats, 4)
            f1 = left(jnp.concatenate([re[:half] - re[half:], im[:half] - im[half:]], axis=0), mats, 6)
            spec[m, 0] = f0
            spec[m, 1] = f1
            factor[0] += f0[:half] * f0[:half] + f0[half:] * f0[half:]
            factor[1] += f1[:half] * f1[:half] + f1[half:] * f1[half:]
            return carry

        lax.fori_loop(0, modes, forward, 0)
        alive = live_ref[p].astype(jnp.float32)
        factor[...] = (1.0 - root[p] / jnp.sqrt(factor[...] + smoothing)) * alive
        placed[...] = jnp.zeros_like(placed)

        def backward(out, first, j, carry):
            group = first // keep
            m = j ^ bit_ref[0] ^ bit_ref[1 + group]
            scale0 = factor[0]
            scale1 = factor[1]
            e = left(spec[m, 0] * jnp.concatenate([scale0, scale0], axis=0), mats, 8)
            o = left(spec[m, 1] * jnp.concatenate([scale1, scale1], axis=0), mats, 10)
            total, other = e + o, e - o
            re = jnp.concatenate([total[:half], other[:half]], axis=0)
            im = jnp.concatenate([total[half:], other[half:]], axis=0)
            even = right(jnp.concatenate([re[:, :half], im[:, :half]], axis=1), mats, 12)
            odd = right(jnp.concatenate([re[:, half:], im[:, half:]], axis=1), mats, 14)
            total, other = even + odd, even - odd
            x_re = jnp.concatenate([total[:, :half], other[:, :half]], axis=1)
            x_im = jnp.concatenate([total[:, half:], other[:, half:]], axis=1)
            q_re, q_im = probe[0, m], probe[1, m]
            placed[0, :width, :width] += q_re * x_re + q_im * x_im
            placed[1, :width, :width] += q_re * x_im - q_im * x_re
            o_re, o_im = patch[0], patch[1]
            gains = (o_re * x_re + o_im * x_im, o_re * x_im - o_im * x_re)
            for c in range(2):
                for h in range(2):
                    down = pl.multiple_of((h ^ bit_ref[5]) * half, half)
                    at = (j - first, c ^ bit_ref[3 + group], pl.ds(down, half))
                    value = gains[c][h * half : (h + 1) * half]
                    if p == 0:
                        out[at] = value
                    else:
                        out[at] = out[at] + value
            return carry

        quarter = modes // 4
        for first, out in ((keep, send0), (0, keep0), (keep + quarter, send1), (quarter, keep1)):
            lax.fori_loop(first, first + quarter, functools.partial(backward, out, first), 0)
        for c in range(2):
            at = (c, pl.ds(top, tall), pl.ds(base, wide))
            grad[at] = grad[at] + pltpu.roll(pltpu.roll(placed[c], drop, 0), shift, 1)

    leaving = [
        pltpu.make_async_copy(src, dst, sems.at[i])
        for i, (src, dst) in enumerate(
            (
                (part(grad, 0, rows, 0, cols), g_own),
                (part(grad, 0, rows, cols, width), g_beside),
                (part(grad, rows, width, 0, cols), g_below),
                (part(grad, rows, width, cols, width), g_corner),
            )
        )
    ]
    for copy in leaving:
        copy.start()
    for copy in leaving:
        copy.wait()


def parity_order(intensity, orders, root):
    half = root.shape[2]

    def parts(x):
        high, low = split(x)
        return high, low, (x - high.astype(jnp.float32) - low.astype(jnp.float32)).astype(jnp.bfloat16)

    for p in range(root.shape[0]):
        high, middle, low = parts(jnp.sqrt(intensity[p]))
        x = dot(orders[0], high) + dot(orders[0], middle) + dot(orders[0], low)
        high, middle, low = parts(x)
        x = dot(high, orders[1]) + dot(middle, orders[1]) + dot(low, orders[1])
        root[p, 0] = x[:half]
        root[p, 1] = x[half:]


def assemble(bit_ref, *refs):
    pieces, out, sems = refs[:-2], refs[-2], refs[-1]
    modes, width = out.shape[1], out.shape[-1]
    half = width // 2
    each = modes // len(pieces)
    copies = []
    for slot in range(modes):
        piece, inner = divmod(slot, each)
        group = slot // (modes // 2)
        m = slot ^ bit_ref[0] ^ bit_ref[1 + group]
        for c in range(2):
            for h in range(2):
                down = pl.multiple_of((h ^ bit_ref[5]) * half, half)
                copies.append(
                    pltpu.make_async_copy(
                        pieces[piece].at[inner, c, pl.ds(h * half, half)],
                        out.at[c ^ bit_ref[3 + group], m, pl.ds(down, half)],
                        sems.at[len(copies)],
                    )
                )
    for copy in copies:
        copy.start()
    for copy in copies:
        copy.wait()


def swap(array, where):
    axis, bit = where
    return lax.ppermute(array, axis, [(i, i ^ (1 << bit)) for i in range(lax.axis_size(axis))])


def bit_of(where):
    axis, bit = where
    return (lax.axis_index(axis) >> bit) & 1


def after(array, earlier):
    return array + 0.0 * earlier.reshape(-1)[0]


def hop(array, turn):
    n_row, n_col = lax.axis_size("row"), lax.axis_size("col")
    pairs = []
    for r in range(n_row):
        for c in range(n_col):
            pairs.append((r * n_col + c, (r ^ (1 << ((turn + c) % 2))) * n_col + c))
    return lax.ppermute(array, ("row", "col"), pairs)


def probe_sum(kept, sent, bits, core, third, rest, below_grad):
    one = kept[0].shape[0] // 2
    half = kept[0].shape[-1] // 2
    totals = []
    for keep, send in zip(kept, sent):
        came = swap(send, core)
        came1 = hop(keep[one:] + came[one:], 0)
        came2 = hop(keep[:one, 1] + came[:one, 1] + came1[:, 1], 1)
        below_grad = after(below_grad, came2)
        totals.append(keep[:one, 0] + came[:one, 0] + came1[:, 0] + came2)
    from_above = passed_along(below_grad, "row", 1)
    own = []
    for number, total in enumerate(totals):
        total = total[:, :half] + swap(total[:, half:], third)
        for where in rest:
            total = total + swap(total, where)
        total = jnp.concatenate([total, swap(total, third)], axis=1)
        if number == 1:
            total = after(total, from_above)
        total = jnp.stack([total, hop(total, 1)], axis=1)
        own += [total, hop(total, 0)]
    pieces = own + [swap(piece, core) for piece in own]
    modes = 4 * kept[0].shape[0]
    width = kept[0].shape[-1]
    probe_grad = pl.pallas_call(
        assemble,
        out_shape=jax.ShapeDtypeStruct((2, modes, width, width), jnp.float32),
        in_specs=[pl.BlockSpec(memory_space=pltpu.SMEM)] + [pl.BlockSpec(memory_space=pltpu.VMEM)] * len(pieces),
        out_specs=pl.BlockSpec(memory_space=pl.ANY),
        scratch_shapes=[pltpu.SemaphoreType.DMA((4 * modes,))],
        compiler_params=pltpu.CompilerParams(vmem_limit_bytes=24 * 1024 * 1024),
    )(bits, *pieces)
    return probe_grad, from_above


def shards(object_field, probe, intensity, row_offset, col_offset, live):
    width = probe.shape[-1]
    modes = probe.shape[1]
    patterns = intensity.shape[0]
    half = width // 2
    rows, cols = object_field.shape[1:]
    row_bits = [("row", i) for i in range(lax.axis_size("row").bit_length() - 1)]
    col_bits = [("col", i) for i in range(lax.axis_size("col").bit_length() - 1)]
    core, x_bit, y_bit = col_bits[0], row_bits[0], row_bits[1]
    others = col_bits[1:] + row_bits[2:]

    below0 = passed_along(object_field[:, :width, :width], "row", -1)
    below1 = passed_along(object_field[:, :width, width:], "row", -1)
    beside = passed_along(object_field[:, :, :width], "col", -1)
    corner = passed_along(below0, "col", -1)
    smem = pl.BlockSpec(memory_space=pltpu.SMEM)
    vmem = pl.BlockSpec(memory_space=pltpu.VMEM)
    hbm = pl.BlockSpec(memory_space=pl.ANY)
    f32 = jnp.float32
    order_rows = np.eye(width)[np.concatenate([np.arange(0, width, 2), np.arange(1, width, 2)])]
    root = pl.pallas_call(
        parity_order,
        out_shape=jax.ShapeDtypeStruct((patterns, 2, half, width), f32),
        in_specs=[vmem, vmem],
        out_specs=vmem,
    )(intensity, jnp.asarray(np.stack([order_rows, order_rows.T]), jnp.bfloat16))
    side, x, y = bit_of(core), bit_of(x_bit), bit_of(y_bit)
    kept_first = jnp.where(side == 0, x, y)
    kept_second = jnp.where(side == 0, y, x)
    eighth = modes // 8
    bits = jnp.stack(
        [side * (modes // 2), kept_first * eighth, kept_second * eighth, kept_second, kept_first, bit_of(others[0])]
    ).astype(jnp.int32)
    mats = jnp.asarray(matrices(width))
    g_own, g_beside, g_below, g_corner, keep0, keep1, send0, send1 = pl.pallas_call(
        kernel,
        out_shape=(
            jax.ShapeDtypeStruct((2, rows, cols), f32),
            jax.ShapeDtypeStruct((2, rows, width), f32),
            jax.ShapeDtypeStruct((2, width, cols), f32),
            jax.ShapeDtypeStruct((2, width, width), f32),
            *[jax.ShapeDtypeStruct((modes // 4, 2, width, width), f32)] * 4,
        ),
        in_specs=[smem] * 4 + [hbm] * 5 + [vmem] * 3,
        out_specs=(*[hbm] * 4, *[vmem] * 4),
        scratch_shapes=[
            pltpu.VMEM((2, rows + width, cols + width), f32),
            pltpu.VMEM((2, rows + width, cols + width), f32),
            pltpu.VMEM((modes, 2, width, width), f32),
            pltpu.VMEM((2, width, width), f32),
            pltpu.VMEM((2, half, width), f32),
            pltpu.VMEM((2, width + 8, width + 128), f32),
            pltpu.SemaphoreType.DMA((5,)),
        ],
        compiler_params=pltpu.CompilerParams(vmem_limit_bytes=48 * 1024 * 1024),
    )(row_offset, col_offset, live, bits, object_field, beside, below0, below1, corner, probe, root, mats)

    below_grad = g_below.at[:, :, :width].add(passed_along(g_corner, "col", 1))
    from_left = passed_along(g_beside, "col", 1)
    probe_grad, from_above = probe_sum(
        (keep0, keep1), (send0, send1), bits, core, others[0], others[1:], below_grad
    )
    object_grad = g_own.at[:, :, :width].add(from_left)
    object_grad = object_grad.at[:, :width, :].add(from_above)
    return (object_grad, probe_grad)


def solution(mesh):
    in_specs = (
        P(None, "row", "col"),
        P(),
        P(("row", "col"), None, None),
        P(("row", "col")),
        P(("row", "col")),
        P(("row", "col")),
    )
    out_specs = (P(None, "row", "col"), P())
    return jax.shard_map(shards, mesh=mesh, in_specs=in_specs, out_specs=out_specs, check_vma=False)
```

```python
import functools

import jax
import jax.numpy as jnp
import ml_dtypes
import numpy as np
from jax import lax
from jax.experimental import pallas as pl
from jax.experimental.pallas import tpu as pltpu
from jax.sharding import PartitionSpec as P

smoothing = 0.25


def passed_along(array, axis, by):
    devices = lax.axis_size(axis)
    pairs = [(i, i + by) for i in range(devices) if 0 <= i + by < devices]
    return lax.ppermute(array, axis, pairs)


def split(x):
    high = x.astype(jnp.bfloat16)
    return high, (x - high.astype(jnp.float32)).astype(jnp.bfloat16)


def matrices(width):
    half = width // 2
    n = np.arange(half)
    scale = 1.0 / np.sqrt(width)
    out = []
    forward_right, forward_left, inverse_left, inverse_right = [], [], [], []
    for parity in (0, 1):
        phase = (n[:, None] * (2 * n[None, :] + parity) % width) * (2.0 * np.pi / width)
        c, s = np.cos(phase) * scale, np.sin(phase) * scale
        forward_right.append(np.block([[c, -s], [s, c]]))
        forward_left.append(np.block([[c.T, s.T], [-s.T, c.T]]))
        inverse_left.append(np.block([[c, -s], [s, c]]))
        inverse_right.append(np.block([[c.T, s.T], [-s.T, c.T]]))
    for pair in (forward_right, forward_left, inverse_left, inverse_right):
        for m in pair:
            high = m.astype(np.float32).astype(ml_dtypes.bfloat16)
            low = (m - high.astype(np.float64)).astype(np.float32).astype(ml_dtypes.bfloat16)
            out.append((high, low))
    rights = [np.concatenate([high, high, low], axis=0) for high, low in out[:2] + out[6:]]
    lefts = [np.concatenate([high, high, low], axis=1) for high, low in out[2:6]]
    return np.stack(rights), np.stack(lefts)


def dot(a, b):
    return jnp.dot(a, b, preferred_element_type=jnp.float32)


def right(z, mats, at):
    high, low = split(z)
    return dot(jnp.concatenate([high, low, high], axis=1), mats[0][at // 2 if at < 4 else at // 2 - 4])


def left(z, mats, at):
    high, low = split(z)
    return dot(mats[1][at // 2 - 2], jnp.concatenate([high, low, high], axis=0))


def kernel(
    row_ref, col_ref, live_ref, bit_ref, own, beside, below0, below1, corner, probe, root, rights, lefts,
    g_own, g_beside, g_below, g_corner, keep0, keep1, send0, send1,
    ext, grad, spec, patch, factor, placed, sems,
):
    mats = (rights, lefts)
    patterns, width = root.shape[0], root.shape[-1]
    modes = probe.shape[1]
    half = width // 2
    rows, cols = own.shape[1], own.shape[2]
    keep = modes // 2

    def part(e, top, height, left_of, wide):
        return e.at[:, pl.ds(top, height), pl.ds(left_of, wide)]

    arriving = [
        pltpu.make_async_copy(src, dst, sems.at[i])
        for i, (src, dst) in enumerate(
            (
                (own, part(ext, 0, rows, 0, cols)),
                (beside, part(ext, 0, rows, cols, width)),
                (below0, part(ext, rows, width, 0, width)),
                (below1, part(ext, rows, width, width, cols - width)),
                (corner, part(ext, rows, width, cols, width)),
            )
        )
    ]
    for copy in arriving:
        copy.start()
    grad[...] = jnp.zeros_like(grad)
    for copy in arriving:
        copy.wait()

    tall, wide = width + 8, width + 128

    def turned(x, by, axis):
        return pltpu.roll(x, jnp.where(by == 0, 0, x.shape[axis] - by), axis)

    corners = []
    for p in range(patterns):
        top = pl.multiple_of((row_ref[p] // 8) * 8, 8)
        drop = row_ref[p] % 8
        base = pl.multiple_of((col_ref[p] // 128) * 128, 128)
        shift = col_ref[p] % 128
        corners.append((top, drop, base, shift))
        for c in range(2):
            window = turned(ext[c, pl.ds(top, tall), pl.ds(base, wide)], drop, 0)[:width]
            patch[p, c] = turned(window, shift, 1)[:, :width]
    factor[...] = jnp.zeros_like(factor)

    def forward(m, carry):
        q_re, q_im = probe[0, m], probe[1, m]
        for p in range(patterns):
            o_re, o_im = patch[p, 0], patch[p, 1]
            e_re = q_re * o_re - q_im * o_im
            e_im = q_re * o_im + q_im * o_re
            r0, r1 = e_re[:, :half], e_re[:, half:]
            i0, i1 = e_im[:, :half], e_im[:, half:]
            even = right(jnp.concatenate([r0 + r1, i0 + i1], axis=1), mats, 0)
            odd = right(jnp.concatenate([r0 - r1, i0 - i1], axis=1), mats, 2)
            re = jnp.concatenate([even[:, :half], odd[:, :half]], axis=1)
            im = jnp.concatenate([even[:, half:], odd[:, half:]], axis=1)
            f0 = left(jnp.concatenate([re[:half] + re[half:], im[:half] + im[half:]], axis=0), mats, 4)
            f1 = left(jnp.concatenate([re[:half] - re[half:], im[:half] - im[half:]], axis=0), mats, 6)
            spec[p, m, 0] = f0
            spec[p, m, 1] = f1
            factor[p, 0] += f0[:half] * f0[:half] + f0[half:] * f0[half:]
            factor[p, 1] += f1[:half] * f1[:half] + f1[half:] * f1[half:]
        return carry

    lax.fori_loop(0, modes, forward, 0, unroll=2)
    for p in range(patterns):
        alive = live_ref[p].astype(jnp.float32)
        factor[p] = (1.0 - root[p] / jnp.sqrt(factor[p] + smoothing)) * alive
    placed[...] = jnp.zeros_like(placed)

    def backward(out, first, j, carry):
        group = first // keep
        m = j ^ bit_ref[0] ^ bit_ref[1 + group]
        q_re, q_im = probe[0, m], probe[1, m]
        gains = [0.0, 0.0]
        for p in range(patterns):
            scale0, scale1 = factor[p, 0], factor[p, 1]
            e = left(spec[p, m, 0] * jnp.concatenate([scale0, scale0], axis=0), mats, 8)
            o = left(spec[p, m, 1] * jnp.concatenate([scale1, scale1], axis=0), mats, 10)
            total, other = e + o, e - o
            re = jnp.concatenate([total[:half], other[:half]], axis=0)
            im = jnp.concatenate([total[half:], other[half:]], axis=0)
            even = right(jnp.concatenate([re[:, :half], im[:, :half]], axis=1), mats, 12)
            odd = right(jnp.concatenate([re[:, half:], im[:, half:]], axis=1), mats, 14)
            total, other = even + odd, even - odd
            x_re = jnp.concatenate([total[:, :half], other[:, :half]], axis=1)
            x_im = jnp.concatenate([total[:, half:], other[:, half:]], axis=1)
            placed[p, 0, :width, :width] += q_re * x_re + q_im * x_im
            placed[p, 1, :width, :width] += q_re * x_im - q_im * x_re
            o_re, o_im = patch[p, 0], patch[p, 1]
            gains[0] += o_re * x_re + o_im * x_im
            gains[1] += o_re * x_im - o_im * x_re
        for c in range(2):
            for h in range(2):
                down = pl.multiple_of((h ^ bit_ref[5]) * half, half)
                at = (j - first, c ^ bit_ref[3 + group], pl.ds(down, half))
                out[at] = gains[c][h * half : (h + 1) * half]
        return carry

    quarter = modes // 4
    for first, out in ((keep, send0), (0, keep0), (keep + quarter, send1), (quarter, keep1)):
        lax.fori_loop(first, first + quarter, functools.partial(backward, out, first), 0, unroll=2)
    for p, (top, drop, base, shift) in enumerate(corners):
        for c in range(2):
            at = (c, pl.ds(top, tall), pl.ds(base, wide))
            grad[at] = grad[at] + pltpu.roll(pltpu.roll(placed[p, c], drop, 0), shift, 1)

    leaving = [
        pltpu.make_async_copy(src, dst, sems.at[i])
        for i, (src, dst) in enumerate(
            (
                (part(grad, 0, rows, 0, cols), g_own),
                (part(grad, 0, rows, cols, width), g_beside),
                (part(grad, rows, width, 0, cols), g_below),
                (part(grad, rows, width, cols, width), g_corner),
            )
        )
    ]
    for copy in leaving:
        copy.start()
    for copy in leaving:
        copy.wait()


def parity_order(intensity, orders, root):
    half = root.shape[2]

    def parts(x):
        high, low = split(x)
        return high, low, (x - high.astype(jnp.float32) - low.astype(jnp.float32)).astype(jnp.bfloat16)

    for p in range(root.shape[0]):
        high, middle, low = parts(jnp.sqrt(intensity[p]))
        x = dot(orders[0], high) + dot(orders[0], middle) + dot(orders[0], low)
        high, middle, low = parts(x)
        x = dot(high, orders[1]) + dot(middle, orders[1]) + dot(low, orders[1])
        root[p, 0] = x[:half]
        root[p, 1] = x[half:]


def assemble(bit_ref, *refs):
    pieces, out, sems = refs[:-2], refs[-2], refs[-1]
    modes, width = out.shape[1], out.shape[-1]
    half = width // 2
    each = modes // len(pieces)
    copies = []
    for slot in range(modes):
        piece, inner = divmod(slot, each)
        group = slot // (modes // 2)
        m = slot ^ bit_ref[0] ^ bit_ref[1 + group]
        for c in range(2):
            for h in range(2):
                down = pl.multiple_of((h ^ bit_ref[5]) * half, half)
                copies.append(
                    pltpu.make_async_copy(
                        pieces[piece].at[inner, c, pl.ds(h * half, half)],
                        out.at[c ^ bit_ref[3 + group], m, pl.ds(down, half)],
                        sems.at[len(copies)],
                    )
                )
    for copy in copies:
        copy.start()
    for copy in copies:
        copy.wait()


def swap(array, where):
    axis, bit = where
    return lax.ppermute(array, axis, [(i, i ^ (1 << bit)) for i in range(lax.axis_size(axis))])


def bit_of(where):
    axis, bit = where
    return (lax.axis_index(axis) >> bit) & 1


def after(array, earlier):
    return array + 0.0 * earlier.reshape(-1)[0]


def hop(array, turn):
    n_row, n_col = lax.axis_size("row"), lax.axis_size("col")
    pairs = []
    for r in range(n_row):
        for c in range(n_col):
            pairs.append((r * n_col + c, (r ^ (1 << ((turn + c) % 2))) * n_col + c))
    return lax.ppermute(array, ("row", "col"), pairs)


def probe_sum(kept, sent, bits, core, third, rest, below_grad):
    one = kept[0].shape[0] // 2
    half = kept[0].shape[-1] // 2
    totals = []
    for keep, send in zip(kept, sent):
        came = swap(send, core)
        came1 = hop(keep[one:] + came[one:], 0)
        came2 = hop(keep[:one, 1] + came[:one, 1] + came1[:, 1], 1)
        below_grad = after(below_grad, came2)
        totals.append(keep[:one, 0] + came[:one, 0] + came1[:, 0] + came2)
    from_above = passed_along(below_grad, "row", 1)
    own = []
    for number, total in enumerate(totals):
        total = total[:, :half] + swap(total[:, half:], third)
        for where in rest:
            total = total + swap(total, where)
        total = jnp.concatenate([total, swap(total, third)], axis=1)
        if number == 1:
            total = after(total, from_above)
        total = jnp.stack([total, hop(total, 1)], axis=1)
        own += [total, hop(total, 0)]
    pieces = own + [swap(piece, core) for piece in own]
    modes = 4 * kept[0].shape[0]
    width = kept[0].shape[-1]
    probe_grad = pl.pallas_call(
        assemble,
        out_shape=jax.ShapeDtypeStruct((2, modes, width, width), jnp.float32),
        in_specs=[pl.BlockSpec(memory_space=pltpu.SMEM)] + [pl.BlockSpec(memory_space=pltpu.VMEM)] * len(pieces),
        out_specs=pl.BlockSpec(memory_space=pl.ANY),
        scratch_shapes=[pltpu.SemaphoreType.DMA((4 * modes,))],
        compiler_params=pltpu.CompilerParams(vmem_limit_bytes=24 * 1024 * 1024),
    )(bits, *pieces)
    return probe_grad, from_above


def shards(object_field, probe, intensity, row_offset, col_offset, live):
    width = probe.shape[-1]
    modes = probe.shape[1]
    patterns = intensity.shape[0]
    half = width // 2
    rows, cols = object_field.shape[1:]
    row_bits = [("row", i) for i in range(lax.axis_size("row").bit_length() - 1)]
    col_bits = [("col", i) for i in range(lax.axis_size("col").bit_length() - 1)]
    core, x_bit, y_bit = col_bits[0], row_bits[0], row_bits[1]
    others = col_bits[1:] + row_bits[2:]

    below0 = passed_along(object_field[:, :width, :width], "row", -1)
    below1 = passed_along(object_field[:, :width, width:], "row", -1)
    beside = passed_along(object_field[:, :, :width], "col", -1)
    corner = passed_along(below0, "col", -1)
    smem = pl.BlockSpec(memory_space=pltpu.SMEM)
    vmem = pl.BlockSpec(memory_space=pltpu.VMEM)
    hbm = pl.BlockSpec(memory_space=pl.ANY)
    f32 = jnp.float32
    order_rows = np.eye(width)[np.concatenate([np.arange(0, width, 2), np.arange(1, width, 2)])]
    root = pl.pallas_call(
        parity_order,
        out_shape=jax.ShapeDtypeStruct((patterns, 2, half, width), f32),
        in_specs=[vmem, vmem],
        out_specs=vmem,
    )(intensity, jnp.asarray(np.stack([order_rows, order_rows.T]), jnp.bfloat16))
    side, x, y = bit_of(core), bit_of(x_bit), bit_of(y_bit)
    kept_first = jnp.where(side == 0, x, y)
    kept_second = jnp.where(side == 0, y, x)
    eighth = modes // 8
    bits = jnp.stack(
        [side * (modes // 2), kept_first * eighth, kept_second * eighth, kept_second, kept_first, bit_of(others[0])]
    ).astype(jnp.int32)
    rights, lefts = matrices(width)
    g_own, g_beside, g_below, g_corner, keep0, keep1, send0, send1 = pl.pallas_call(
        kernel,
        out_shape=(
            jax.ShapeDtypeStruct((2, rows, cols), f32),
            jax.ShapeDtypeStruct((2, rows, width), f32),
            jax.ShapeDtypeStruct((2, width, cols), f32),
            jax.ShapeDtypeStruct((2, width, width), f32),
            *[jax.ShapeDtypeStruct((modes // 4, 2, width, width), f32)] * 4,
        ),
        in_specs=[smem] * 4 + [hbm] * 5 + [vmem] * 4,
        out_specs=(*[hbm] * 4, *[vmem] * 4),
        scratch_shapes=[
            pltpu.VMEM((2, rows + width, cols + width), f32),
            pltpu.VMEM((2, rows + width, cols + width), f32),
            pltpu.VMEM((patterns, modes, 2, width, width), f32),
            pltpu.VMEM((patterns, 2, width, width), f32),
            pltpu.VMEM((patterns, 2, half, width), f32),
            pltpu.VMEM((patterns, 2, width + 8, width + 128), f32),
            pltpu.SemaphoreType.DMA((5,)),
        ],
        compiler_params=pltpu.CompilerParams(vmem_limit_bytes=48 * 1024 * 1024),
    )(row_offset, col_offset, live, bits, object_field, beside, below0, below1, corner, probe, root, jnp.asarray(rights), jnp.asarray(lefts))

    below_grad = g_below.at[:, :, :width].add(passed_along(g_corner, "col", 1))
    from_left = passed_along(g_beside, "col", 1)
    probe_grad, from_above = probe_sum(
        (keep0, keep1), (send0, send1), bits, core, others[0], others[1:], below_grad
    )
    object_grad = g_own.at[:, :, :width].add(from_left)
    object_grad = object_grad.at[:, :width, :].add(from_above)
    return (object_grad, probe_grad)


def solution(mesh):
    in_specs = (
        P(None, "row", "col"),
        P(),
        P(("row", "col"), None, None),
        P(("row", "col")),
        P(("row", "col")),
        P(("row", "col")),
    )
    out_specs = (P(None, "row", "col"), P())
    return jax.shard_map(shards, mesh=mesh, in_specs=in_specs, out_specs=out_specs, check_vma=False)
```

```python
import functools

import jax
import jax.numpy as jnp
import ml_dtypes
import numpy as np
from jax import lax
from jax.experimental import pallas as pl
from jax.experimental.pallas import tpu as pltpu
from jax.sharding import PartitionSpec as P

smoothing = 0.25


def passed_along(array, axis, by):
    devices = lax.axis_size(axis)
    pairs = [(i, i + by) for i in range(devices) if 0 <= i + by < devices]
    return lax.ppermute(array, axis, pairs)


def split(x):
    high = x.astype(jnp.bfloat16)
    return high, (x - high.astype(jnp.float32)).astype(jnp.bfloat16)


def matrices(width):
    half = width // 2
    n = np.arange(half)
    scale = 1.0 / np.sqrt(width)
    out = []
    forward_right, forward_left, inverse_left, inverse_right = [], [], [], []
    for parity in (0, 1):
        phase = (n[:, None] * (2 * n[None, :] + parity) % width) * (2.0 * np.pi / width)
        c, s = np.cos(phase) * scale, np.sin(phase) * scale
        forward_right.append(np.block([[c, -s], [s, c]]))
        forward_left.append(np.block([[c.T, s.T], [-s.T, c.T]]))
        inverse_left.append(np.block([[c, -s], [s, c]]))
        inverse_right.append(np.block([[c.T, s.T], [-s.T, c.T]]))
    for pair in (forward_right, forward_left, inverse_left, inverse_right):
        for m in pair:
            high = m.astype(np.float32).astype(ml_dtypes.bfloat16)
            low = (m - high.astype(np.float64)).astype(np.float32).astype(ml_dtypes.bfloat16)
            out.append((high, low))
    rights = [np.concatenate([high, high, low], axis=0) for high, low in out[:2] + out[6:]]
    lefts = [np.concatenate([high, high, low], axis=1) for high, low in out[2:6]]
    return np.stack(rights), np.stack(lefts)


def dot(a, b):
    return jnp.dot(a, b, preferred_element_type=jnp.float32)


def right(z, mats, at):
    high, low = split(z)
    return dot(jnp.concatenate([high, low, high], axis=1), mats[0][at // 2 if at < 4 else at // 2 - 4])


def left(z, mats, at):
    high, low = split(z)
    return dot(mats[1][at // 2 - 2], jnp.concatenate([high, low, high], axis=0))


def kernel(
    row_ref, col_ref, live_ref, bit_ref, own, beside, below0, below1, corner, probe_in, root_in, rights, lefts,
    g_own, g_beside, g_below, g_corner, keep0, keep1, send0, send1,
    ext, grad, spec, patch, factor, placed, probe, root, sems, probe_sems,
):
    mats = (rights, lefts)
    patterns, width = root.shape[0], root.shape[-1]
    modes = probe.shape[1]
    half = width // 2
    rows, cols = own.shape[1], own.shape[2]
    keep = modes // 2

    def part(e, top, height, left_of, wide):
        return e.at[:, pl.ds(top, height), pl.ds(left_of, wide)]

    arriving = [
        pltpu.make_async_copy(src, dst, sems.at[i])
        for i, (src, dst) in enumerate(
            (
                (own, part(ext, 0, rows, 0, cols)),
                (beside, part(ext, 0, rows, cols, width)),
                (below0, part(ext, rows, width, 0, width)),
                (below1, part(ext, rows, width, width, cols - width)),
                (corner, part(ext, rows, width, cols, width)),
            )
        )
    ]
    for copy in arriving:
        copy.start()

    def mode_copy(m):
        return pltpu.make_async_copy(probe_in.at[:, m], probe.at[:, m], probe_sems.at[m])

    for m in range(modes):
        mode_copy(m).start()
    root_copy = pltpu.make_async_copy(root_in, root, sems.at[5])
    root_copy.start()
    grad[...] = jnp.zeros_like(grad)
    for copy in arriving:
        copy.wait()

    tall, wide = width + 8, width + 128

    def turned(x, by, axis):
        return pltpu.roll(x, jnp.where(by == 0, 0, x.shape[axis] - by), axis)

    corners = []
    for p in range(patterns):
        top = pl.multiple_of((row_ref[p] // 8) * 8, 8)
        drop = row_ref[p] % 8
        base = pl.multiple_of((col_ref[p] // 128) * 128, 128)
        shift = col_ref[p] % 128
        corners.append((top, drop, base, shift))
        for c in range(2):
            window = turned(ext[c, pl.ds(top, tall), pl.ds(base, wide)], drop, 0)[:width]
            patch[p, c] = turned(window, shift, 1)[:, :width]
    factor[...] = jnp.zeros_like(factor)

    def forward(m, carry):
        mode_copy(m).wait()
        q_re, q_im = probe[0, m], probe[1, m]
        for p in range(patterns):
            o_re, o_im = patch[p, 0], patch[p, 1]
            e_re = q_re * o_re - q_im * o_im
            e_im = q_re * o_im + q_im * o_re
            r0, r1 = e_re[:, :half], e_re[:, half:]
            i0, i1 = e_im[:, :half], e_im[:, half:]
            even = right(jnp.concatenate([r0 + r1, i0 + i1], axis=1), mats, 0)
            odd = right(jnp.concatenate([r0 - r1, i0 - i1], axis=1), mats, 2)
            re = jnp.concatenate([even[:, :half], odd[:, :half]], axis=1)
            im = jnp.concatenate([even[:, half:], odd[:, half:]], axis=1)
            f0 = left(jnp.concatenate([re[:half] + re[half:], im[:half] + im[half:]], axis=0), mats, 4)
            f1 = left(jnp.concatenate([re[:half] - re[half:], im[:half] - im[half:]], axis=0), mats, 6)
            spec[p, m, 0] = f0
            spec[p, m, 1] = f1
            factor[p, 0] += f0[:half] * f0[:half] + f0[half:] * f0[half:]
            factor[p, 1] += f1[:half] * f1[:half] + f1[half:] * f1[half:]
        return carry

    lax.fori_loop(0, modes, forward, 0, unroll=2)
    root_copy.wait()
    for p in range(patterns):
        alive = live_ref[p].astype(jnp.float32)
        factor[p] = (1.0 - root[p] / jnp.sqrt(factor[p] + smoothing)) * alive
    placed[...] = jnp.zeros_like(placed)

    def backward(out, first, j, carry):
        group = first // keep
        m = j ^ bit_ref[0] ^ bit_ref[1 + group]
        q_re, q_im = probe[0, m], probe[1, m]
        gains = [0.0, 0.0]
        for p in range(patterns):
            scale0, scale1 = factor[p, 0], factor[p, 1]
            e = left(spec[p, m, 0] * jnp.concatenate([scale0, scale0], axis=0), mats, 8)
            o = left(spec[p, m, 1] * jnp.concatenate([scale1, scale1], axis=0), mats, 10)
            total, other = e + o, e - o
            re = jnp.concatenate([total[:half], other[:half]], axis=0)
            im = jnp.concatenate([total[half:], other[half:]], axis=0)
            even = right(jnp.concatenate([re[:, :half], im[:, :half]], axis=1), mats, 12)
            odd = right(jnp.concatenate([re[:, half:], im[:, half:]], axis=1), mats, 14)
            total, other = even + odd, even - odd
            x_re = jnp.concatenate([total[:, :half], other[:, :half]], axis=1)
            x_im = jnp.concatenate([total[:, half:], other[:, half:]], axis=1)
            placed[p, 0, :width, :width] += q_re * x_re + q_im * x_im
            placed[p, 1, :width, :width] += q_re * x_im - q_im * x_re
            o_re, o_im = patch[p, 0], patch[p, 1]
            gains[0] += o_re * x_re + o_im * x_im
            gains[1] += o_re * x_im - o_im * x_re
        for c in range(2):
            for h in range(2):
                down = pl.multiple_of((h ^ bit_ref[5]) * half, half)
                at = (j - first, c ^ bit_ref[3 + group], pl.ds(down, half))
                out[at] = gains[c][h * half : (h + 1) * half]
        return carry

    quarter = modes // 4
    for first, out in ((keep, send0), (0, keep0), (keep + quarter, send1), (quarter, keep1)):
        lax.fori_loop(first, first + quarter, functools.partial(backward, out, first), 0, unroll=2)
    for p, (top, drop, base, shift) in enumerate(corners):
        for c in range(2):
            at = (c, pl.ds(top, tall), pl.ds(base, wide))
            grad[at] = grad[at] + pltpu.roll(pltpu.roll(placed[p, c], drop, 0), shift, 1)

    leaving = [
        pltpu.make_async_copy(src, dst, sems.at[i])
        for i, (src, dst) in enumerate(
            (
                (part(grad, 0, rows, 0, cols), g_own),
                (part(grad, 0, rows, cols, width), g_beside),
                (part(grad, rows, width, 0, cols), g_below),
                (part(grad, rows, width, cols, width), g_corner),
            )
        )
    ]
    for copy in leaving:
        copy.start()
    for copy in leaving:
        copy.wait()


def parity_order(intensity, orders, root):
    half = root.shape[2]

    def parts(x):
        high, low = split(x)
        return high, low, (x - high.astype(jnp.float32) - low.astype(jnp.float32)).astype(jnp.bfloat16)

    for p in range(root.shape[0]):
        high, middle, low = parts(jnp.sqrt(intensity[p]))
        x = dot(orders[0], high) + dot(orders[0], middle) + dot(orders[0], low)
        high, middle, low = parts(x)
        x = dot(high, orders[1]) + dot(middle, orders[1]) + dot(low, orders[1])
        root[p, 0] = x[:half]
        root[p, 1] = x[half:]


def assemble(bit_ref, *refs):
    pieces, out, sems = refs[:-2], refs[-2], refs[-1]
    modes, width = out.shape[1], out.shape[-1]
    half = width // 2
    each = modes // len(pieces)
    copies = []
    for slot in range(modes):
        piece, inner = divmod(slot, each)
        group = slot // (modes // 2)
        m = slot ^ bit_ref[0] ^ bit_ref[1 + group]
        for c in range(2):
            for h in range(2):
                down = pl.multiple_of((h ^ bit_ref[5]) * half, half)
                copies.append(
                    pltpu.make_async_copy(
                        pieces[piece].at[inner, c, pl.ds(h * half, half)],
                        out.at[c ^ bit_ref[3 + group], m, pl.ds(down, half)],
                        sems.at[len(copies)],
                    )
                )
    for copy in copies:
        copy.start()
    for copy in copies:
        copy.wait()


def swap(array, where):
    axis, bit = where
    return lax.ppermute(array, axis, [(i, i ^ (1 << bit)) for i in range(lax.axis_size(axis))])


def bit_of(where):
    axis, bit = where
    return (lax.axis_index(axis) >> bit) & 1


def after(array, earlier):
    return array + 0.0 * earlier.reshape(-1)[0]


def hop(array, turn):
    n_row, n_col = lax.axis_size("row"), lax.axis_size("col")
    pairs = []
    for r in range(n_row):
        for c in range(n_col):
            pairs.append((r * n_col + c, (r ^ (1 << ((turn + c) % 2))) * n_col + c))
    return lax.ppermute(array, ("row", "col"), pairs)


def probe_sum(kept, sent, bits, core, third, rest, below_grad, from_left):
    one = kept[0].shape[0] // 2
    half = kept[0].shape[-1] // 2
    totals = []
    for keep, send in zip(kept, sent):
        came = swap(send, core)
        came1 = hop(keep[one:] + came[one:], 0)
        came2 = hop(keep[:one, 1] + came[:one, 1] + came1[:, 1], 1)
        below_grad = after(below_grad, came2)
        totals.append(keep[:one, 0] + came[:one, 0] + came1[:, 0] + came2)
    from_above = passed_along(below_grad, "row", 1)
    own = []
    totals[0] = after(totals[0], from_left)
    for number, total in enumerate(totals):
        total = total[:, :half] + swap(total[:, half:], third)
        for where in rest:
            total = total + swap(total, where)
        total = jnp.concatenate([total, swap(total, third)], axis=1)
        if number == 1:
            total = after(total, from_above)
        total = jnp.stack([total, hop(total, 1)], axis=1)
        own += [total, hop(total, 0)]
    pieces = own + [swap(piece, core) for piece in own]
    modes = 4 * kept[0].shape[0]
    width = kept[0].shape[-1]
    probe_grad = pl.pallas_call(
        assemble,
        out_shape=jax.ShapeDtypeStruct((2, modes, width, width), jnp.float32),
        in_specs=[pl.BlockSpec(memory_space=pltpu.SMEM)] + [pl.BlockSpec(memory_space=pltpu.VMEM)] * len(pieces),
        out_specs=pl.BlockSpec(memory_space=pl.ANY),
        scratch_shapes=[pltpu.SemaphoreType.DMA((4 * modes,))],
        compiler_params=pltpu.CompilerParams(vmem_limit_bytes=24 * 1024 * 1024),
    )(bits, *pieces)
    return probe_grad, from_above


def shards(object_field, probe, intensity, row_offset, col_offset, live):
    width = probe.shape[-1]
    modes = probe.shape[1]
    patterns = intensity.shape[0]
    half = width // 2
    rows, cols = object_field.shape[1:]
    row_bits = [("row", i) for i in range(lax.axis_size("row").bit_length() - 1)]
    col_bits = [("col", i) for i in range(lax.axis_size("col").bit_length() - 1)]
    core, x_bit, y_bit = col_bits[0], row_bits[0], row_bits[1]
    others = col_bits[1:] + row_bits[2:]

    below0 = passed_along(object_field[:, :width, :width], "row", -1)
    below1 = passed_along(object_field[:, :width, width:], "row", -1)
    beside = passed_along(object_field[:, :, :width], "col", -1)
    corner = passed_along(below0, "col", -1)
    smem = pl.BlockSpec(memory_space=pltpu.SMEM)
    vmem = pl.BlockSpec(memory_space=pltpu.VMEM)
    hbm = pl.BlockSpec(memory_space=pl.ANY)
    f32 = jnp.float32
    order_rows = np.eye(width)[np.concatenate([np.arange(0, width, 2), np.arange(1, width, 2)])]
    root = pl.pallas_call(
        parity_order,
        out_shape=jax.ShapeDtypeStruct((patterns, 2, half, width), f32),
        in_specs=[vmem, vmem],
        out_specs=vmem,
    )(intensity, jnp.asarray(np.stack([order_rows, order_rows.T]), jnp.bfloat16))
    side, x, y = bit_of(core), bit_of(x_bit), bit_of(y_bit)
    kept_first = jnp.where(side == 0, x, y)
    kept_second = jnp.where(side == 0, y, x)
    eighth = modes // 8
    bits = jnp.stack(
        [side * (modes // 2), kept_first * eighth, kept_second * eighth, kept_second, kept_first, bit_of(others[0])]
    ).astype(jnp.int32)
    rights, lefts = matrices(width)
    g_own, g_beside, g_below, g_corner, keep0, keep1, send0, send1 = pl.pallas_call(
        kernel,
        out_shape=(
            jax.ShapeDtypeStruct((2, rows, cols), f32),
            jax.ShapeDtypeStruct((2, rows, width), f32),
            jax.ShapeDtypeStruct((2, width, cols), f32),
            jax.ShapeDtypeStruct((2, width, width), f32),
            *[jax.ShapeDtypeStruct((modes // 4, 2, width, width), f32)] * 4,
        ),
        in_specs=[smem] * 4 + [hbm] * 7 + [vmem] * 2,
        out_specs=(*[hbm] * 4, *[vmem] * 4),
        scratch_shapes=[
            pltpu.VMEM((2, rows + width, cols + width), f32),
            pltpu.VMEM((2, rows + width, cols + width), f32),
            pltpu.VMEM((patterns, modes, 2, width, width), f32),
            pltpu.VMEM((patterns, 2, width, width), f32),
            pltpu.VMEM((patterns, 2, half, width), f32),
            pltpu.VMEM((patterns, 2, width + 8, width + 128), f32),
            pltpu.VMEM(probe.shape, f32),
            pltpu.VMEM((patterns, 2, half, width), f32),
            pltpu.SemaphoreType.DMA((6,)),
            pltpu.SemaphoreType.DMA((modes,)),
        ],
        compiler_params=pltpu.CompilerParams(vmem_limit_bytes=48 * 1024 * 1024),
    )(row_offset, col_offset, live, bits, object_field, beside, below0, below1, corner, probe, root, jnp.asarray(rights), jnp.asarray(lefts))

    below_grad = g_below.at[:, :, :width].add(passed_along(g_corner, "col", 1))
    from_left = passed_along(g_beside, "col", 1)
    probe_grad, from_above = probe_sum(
        (keep0, keep1), (send0, send1), bits, core, others[0], others[1:], below_grad, from_left
    )
    object_grad = g_own.at[:, :, :width].add(from_left)
    object_grad = object_grad.at[:, :width, :].add(from_above)
    return (object_grad, probe_grad)


def solution(mesh):
    in_specs = (
        P(None, "row", "col"),
        P(),
        P(("row", "col"), None, None),
        P(("row", "col")),
        P(("row", "col")),
        P(("row", "col")),
    )
    out_specs = (P(None, "row", "col"), P())
    return jax.shard_map(shards, mesh=mesh, in_specs=in_specs, out_specs=out_specs, check_vma=False)
```

```python
import functools

import jax
import jax.numpy as jnp
import ml_dtypes
import numpy as np
from jax import lax
from jax.experimental import pallas as pl
from jax.experimental.pallas import tpu as pltpu
from jax.sharding import PartitionSpec as P

smoothing = 0.25


def passed_along(array, axis, by):
    devices = lax.axis_size(axis)
    pairs = [(i, i + by) for i in range(devices) if 0 <= i + by < devices]
    return lax.ppermute(array, axis, pairs)


def split(x):
    high = x.astype(jnp.bfloat16)
    return high, (x - high.astype(jnp.float32)).astype(jnp.bfloat16)


def matrices(width):
    half = width // 2
    n = np.arange(half)
    scale = 1.0 / np.sqrt(width)
    out = []
    forward_right, forward_left, inverse_left, inverse_right = [], [], [], []
    for parity in (0, 1):
        phase = (n[:, None] * (2 * n[None, :] + parity) % width) * (2.0 * np.pi / width)
        c, s = np.cos(phase) * scale, np.sin(phase) * scale
        forward_right.append(np.block([[c, -s], [s, c]]))
        forward_left.append(np.block([[c.T, s.T], [-s.T, c.T]]))
        inverse_left.append(np.block([[c, -s], [s, c]]))
        inverse_right.append(np.block([[c.T, s.T], [-s.T, c.T]]))
    for pair in (forward_right, forward_left, inverse_left, inverse_right):
        for m in pair:
            high = m.astype(np.float32).astype(ml_dtypes.bfloat16)
            low = (m - high.astype(np.float64)).astype(np.float32).astype(ml_dtypes.bfloat16)
            out.append((high, low))
    rights = [np.concatenate([high, high, low], axis=0) for high, low in out[:2] + out[6:]]
    lefts = [np.concatenate([high, high, low], axis=1) for high, low in out[2:6]]
    return np.stack(rights), np.stack(lefts)


def dot(a, b):
    return jnp.dot(a, b, preferred_element_type=jnp.float32)


def right(z, mats, at):
    high, low = split(z)
    return dot(jnp.concatenate([high, low, high], axis=1), mats[0][at // 2 if at < 4 else at // 2 - 4])


def left(z, mats, at):
    high, low = split(z)
    return dot(mats[1][at // 2 - 2], jnp.concatenate([high, low, high], axis=0))


def kernel(
    row_ref, col_ref, live_ref, bit_ref, own, beside, below0, below1, corner, probe_in, root_in, rights, lefts,
    g_own, g_beside, g_below, g_corner, keep0, keep1, send0, send1,
    ext, grad, spec, patch, factor, placed, probe, root, sems, probe_sems,
):
    mats = (rights, lefts)
    patterns, width = root.shape[0], root.shape[-1]
    modes = probe.shape[1]
    half = width // 2
    rows, cols = own.shape[1], own.shape[2]
    keep = modes // 2

    def part(e, top, height, left_of, wide):
        return e.at[:, pl.ds(top, height), pl.ds(left_of, wide)]

    arriving = [
        pltpu.make_async_copy(src, dst, sems.at[i])
        for i, (src, dst) in enumerate(
            (
                (own, part(ext, 0, rows, 0, cols)),
                (beside, part(ext, 0, rows, cols, width)),
                (below0, part(ext, rows, width, 0, width)),
                (below1, part(ext, rows, width, width, cols - width)),
                (corner, part(ext, rows, width, cols, width)),
            )
        )
    ]
    for copy in arriving:
        copy.start()

    def mode_copy(m):
        return pltpu.make_async_copy(probe_in.at[:, m], probe.at[:, m], probe_sems.at[m])

    for m in range(modes):
        mode_copy(m).start()
    root_copy = pltpu.make_async_copy(root_in, root, sems.at[5])
    root_copy.start()
    grad[...] = jnp.zeros_like(grad)
    for copy in arriving:
        copy.wait()

    tall, wide = width + 8, width + 128

    def turned(x, by, axis):
        return pltpu.roll(x, jnp.where(by == 0, 0, x.shape[axis] - by), axis)

    corners = []
    for p in range(patterns):
        top = pl.multiple_of((row_ref[p] // 8) * 8, 8)
        drop = row_ref[p] % 8
        base = pl.multiple_of((col_ref[p] // 128) * 128, 128)
        shift = col_ref[p] % 128
        corners.append((top, drop, base, shift))
        for c in range(2):
            window = turned(ext[c, pl.ds(top, tall), pl.ds(base, wide)], drop, 0)[:width]
            patch[p, c] = turned(window, shift, 1)[:, :width]
    factor[...] = jnp.zeros_like(factor)

    def forward(m, carry):
        mode_copy(m).wait()
        q_re, q_im = probe[0, m], probe[1, m]
        for p in range(patterns):
            o_re, o_im = patch[p, 0], patch[p, 1]
            e_re = q_re * o_re - q_im * o_im
            e_im = q_re * o_im + q_im * o_re
            r0, r1 = e_re[:, :half], e_re[:, half:]
            i0, i1 = e_im[:, :half], e_im[:, half:]
            even = right(jnp.concatenate([r0 + r1, i0 + i1], axis=1), mats, 0)
            odd = right(jnp.concatenate([r0 - r1, i0 - i1], axis=1), mats, 2)
            re = jnp.concatenate([even[:, :half], odd[:, :half]], axis=1)
            im = jnp.concatenate([even[:, half:], odd[:, half:]], axis=1)
            f0 = left(jnp.concatenate([re[:half] + re[half:], im[:half] + im[half:]], axis=0), mats, 4)
            f1 = left(jnp.concatenate([re[:half] - re[half:], im[:half] - im[half:]], axis=0), mats, 6)
            spec[p, m, 0] = f0
            spec[p, m, 1] = f1
            factor[p, 0] += f0[:half] * f0[:half] + f0[half:] * f0[half:]
            factor[p, 1] += f1[:half] * f1[:half] + f1[half:] * f1[half:]
        return carry

    lax.fori_loop(0, modes, forward, 0, unroll=2)
    root_copy.wait()
    for p in range(patterns):
        alive = live_ref[p].astype(jnp.float32)
        factor[p] = (1.0 - root[p] / jnp.sqrt(factor[p] + smoothing)) * alive
    placed[...] = jnp.zeros_like(placed)

    def backward(out, first, j, carry):
        group = first // keep
        m = j ^ bit_ref[0] ^ bit_ref[1 + group]
        q_re, q_im = probe[0, m], probe[1, m]
        gains = [0.0, 0.0]
        for p in range(patterns):
            scale0, scale1 = factor[p, 0], factor[p, 1]
            e = left(spec[p, m, 0] * jnp.concatenate([scale0, scale0], axis=0), mats, 8)
            o = left(spec[p, m, 1] * jnp.concatenate([scale1, scale1], axis=0), mats, 10)
            total, other = e + o, e - o
            re = jnp.concatenate([total[:half], other[:half]], axis=0)
            im = jnp.concatenate([total[half:], other[half:]], axis=0)
            even = right(jnp.concatenate([re[:, :half], im[:, :half]], axis=1), mats, 12)
            odd = right(jnp.concatenate([re[:, half:], im[:, half:]], axis=1), mats, 14)
            total, other = even + odd, even - odd
            x_re = jnp.concatenate([total[:, :half], other[:, :half]], axis=1)
            x_im = jnp.concatenate([total[:, half:], other[:, half:]], axis=1)
            placed[p, 0, :width, :width] += q_re * x_re + q_im * x_im
            placed[p, 1, :width, :width] += q_re * x_im - q_im * x_re
            o_re, o_im = patch[p, 0], patch[p, 1]
            gains[0] += o_re * x_re + o_im * x_im
            gains[1] += o_re * x_im - o_im * x_re
        for c in range(2):
            for h in range(2):
                down = pl.multiple_of((h ^ bit_ref[5]) * half, half)
                at = (j - first, c ^ bit_ref[3 + group], pl.ds(down, half))
                out[at] = gains[c][h * half : (h + 1) * half]
        return carry

    quarter = modes // 4
    for first, out in ((keep, send0), (0, keep0), (keep + quarter, send1), (quarter, keep1)):
        lax.fori_loop(first, first + quarter, functools.partial(backward, out, first), 0, unroll=2)
    for p, (top, drop, base, shift) in enumerate(corners):
        for c in range(2):
            at = (c, pl.ds(top, tall), pl.ds(base, wide))
            grad[at] = grad[at] + pltpu.roll(pltpu.roll(placed[p, c], drop, 0), shift, 1)

    leaving = [
        pltpu.make_async_copy(src, dst, sems.at[i])
        for i, (src, dst) in enumerate(
            (
                (part(grad, 0, rows, 0, cols), g_own),
                (part(grad, 0, rows, cols, width), g_beside),
                (part(grad, rows, width, 0, cols), g_below),
                (part(grad, rows, width, cols, width), g_corner),
            )
        )
    ]
    for copy in leaving:
        copy.start()
    for copy in leaving:
        copy.wait()


def parity_order(intensity, orders, root):
    half = root.shape[2]

    def parts(x):
        high, low = split(x)
        return high, low, (x - high.astype(jnp.float32) - low.astype(jnp.float32)).astype(jnp.bfloat16)

    for p in range(root.shape[0]):
        high, middle, low = parts(jnp.sqrt(intensity[p]))
        x = dot(orders[0], high) + dot(orders[0], middle) + dot(orders[0], low)
        high, middle, low = parts(x)
        x = dot(high, orders[1]) + dot(middle, orders[1]) + dot(low, orders[1])
        root[p, 0] = x[:half]
        root[p, 1] = x[half:]


def assemble(bit_ref, *refs):
    pieces, out, sems = refs[:-2], refs[-2], refs[-1]
    modes, width = out.shape[1], out.shape[-1]
    half = width // 2
    each = modes // len(pieces)
    copies = []
    for slot in range(modes):
        piece, inner = divmod(slot, each)
        group = slot // (modes // 2)
        m = slot ^ bit_ref[0] ^ bit_ref[1 + group]
        for c in range(2):
            for h in range(2):
                down = pl.multiple_of((h ^ bit_ref[5]) * half, half)
                copies.append(
                    pltpu.make_async_copy(
                        pieces[piece].at[inner, c, pl.ds(h * half, half)],
                        out.at[c ^ bit_ref[3 + group], m, pl.ds(down, half)],
                        sems.at[len(copies)],
                    )
                )
    for copy in copies:
        copy.start()
    for copy in copies:
        copy.wait()


def swap(array, where):
    axis, bit = where
    return lax.ppermute(array, axis, [(i, i ^ (1 << bit)) for i in range(lax.axis_size(axis))])


def bit_of(where):
    axis, bit = where
    return (lax.axis_index(axis) >> bit) & 1


def after(array, earlier):
    return array + 0.0 * earlier.reshape(-1)[0]


def hop(array, turn):
    n_row, n_col = lax.axis_size("row"), lax.axis_size("col")
    pairs = []
    for r in range(n_row):
        for c in range(n_col):
            pairs.append((r * n_col + c, (r ^ (1 << ((turn + c) % 2))) * n_col + c))
    return lax.ppermute(array, ("row", "col"), pairs)


def probe_sum(kept, sent, bits, core, third, rest, below_grad, from_left):
    one = kept[0].shape[0] // 2
    half = kept[0].shape[-1] // 2
    totals = []
    for keep, send in zip(kept, sent):
        came = swap(send, core)
        came1 = hop(keep[one:] + came[one:], 0)
        came2 = hop(keep[:one, 1] + came[:one, 1] + came1[:, 1], 1)
        below_grad = after(below_grad, came2)
        totals.append(keep[:one, 0] + came[:one, 0] + came1[:, 0] + came2)
    from_above = passed_along(below_grad, "row", 1)
    own = []
    totals[1] = after(totals[1], from_left)
    for number, total in enumerate(totals):
        total = total[:, :half] + swap(total[:, half:], third)
        for where in rest:
            total = total + swap(total, where)
        total = jnp.concatenate([total, swap(total, third)], axis=1)
        if number == 1:
            total = after(total, from_above)
        total = jnp.stack([total, hop(total, 1)], axis=1)
        own += [total, hop(total, 0)]
    pieces = own + [swap(piece, core) for piece in own]
    modes = 4 * kept[0].shape[0]
    width = kept[0].shape[-1]
    probe_grad = pl.pallas_call(
        assemble,
        out_shape=jax.ShapeDtypeStruct((2, modes, width, width), jnp.float32),
        in_specs=[pl.BlockSpec(memory_space=pltpu.SMEM)] + [pl.BlockSpec(memory_space=pltpu.VMEM)] * len(pieces),
        out_specs=pl.BlockSpec(memory_space=pl.ANY),
        scratch_shapes=[pltpu.SemaphoreType.DMA((4 * modes,))],
        compiler_params=pltpu.CompilerParams(vmem_limit_bytes=24 * 1024 * 1024),
    )(bits, *pieces)
    return probe_grad, from_above


def shards(object_field, probe, intensity, row_offset, col_offset, live):
    width = probe.shape[-1]
    modes = probe.shape[1]
    patterns = intensity.shape[0]
    half = width // 2
    rows, cols = object_field.shape[1:]
    row_bits = [("row", i) for i in range(lax.axis_size("row").bit_length() - 1)]
    col_bits = [("col", i) for i in range(lax.axis_size("col").bit_length() - 1)]
    core, x_bit, y_bit = col_bits[0], row_bits[0], row_bits[1]
    others = col_bits[1:] + row_bits[2:]

    below0 = passed_along(object_field[:, :width, :width], "row", -1)
    below1 = passed_along(object_field[:, :width, width:], "row", -1)
    beside = passed_along(object_field[:, :, :width], "col", -1)
    corner = passed_along(below0, "col", -1)
    smem = pl.BlockSpec(memory_space=pltpu.SMEM)
    vmem = pl.BlockSpec(memory_space=pltpu.VMEM)
    hbm = pl.BlockSpec(memory_space=pl.ANY)
    f32 = jnp.float32
    order_rows = np.eye(width)[np.concatenate([np.arange(0, width, 2), np.arange(1, width, 2)])]
    root = pl.pallas_call(
        parity_order,
        out_shape=jax.ShapeDtypeStruct((patterns, 2, half, width), f32),
        in_specs=[vmem, vmem],
        out_specs=vmem,
    )(intensity, jnp.asarray(np.stack([order_rows, order_rows.T]), jnp.bfloat16))
    side, x, y = bit_of(core), bit_of(x_bit), bit_of(y_bit)
    kept_first = jnp.where(side == 0, x, y)
    kept_second = jnp.where(side == 0, y, x)
    eighth = modes // 8
    bits = jnp.stack(
        [side * (modes // 2), kept_first * eighth, kept_second * eighth, kept_second, kept_first, bit_of(others[0])]
    ).astype(jnp.int32)
    rights, lefts = matrices(width)
    g_own, g_beside, g_below, g_corner, keep0, keep1, send0, send1 = pl.pallas_call(
        kernel,
        out_shape=(
            jax.ShapeDtypeStruct((2, rows, cols), f32),
            jax.ShapeDtypeStruct((2, rows, width), f32),
            jax.ShapeDtypeStruct((2, width, cols), f32),
            jax.ShapeDtypeStruct((2, width, width), f32),
            *[jax.ShapeDtypeStruct((modes // 4, 2, width, width), f32)] * 4,
        ),
        in_specs=[smem] * 4 + [hbm] * 7 + [vmem] * 2,
        out_specs=(*[hbm] * 4, *[vmem] * 4),
        scratch_shapes=[
            pltpu.VMEM((2, rows + width, cols + width), f32),
            pltpu.VMEM((2, rows + width, cols + width), f32),
            pltpu.VMEM((patterns, modes, 2, width, width), f32),
            pltpu.VMEM((patterns, 2, width, width), f32),
            pltpu.VMEM((patterns, 2, half, width), f32),
            pltpu.VMEM((patterns, 2, width + 8, width + 128), f32),
            pltpu.VMEM(probe.shape, f32),
            pltpu.VMEM((patterns, 2, half, width), f32),
            pltpu.SemaphoreType.DMA((6,)),
            pltpu.SemaphoreType.DMA((modes,)),
        ],
        compiler_params=pltpu.CompilerParams(vmem_limit_bytes=48 * 1024 * 1024),
    )(row_offset, col_offset, live, bits, object_field, beside, below0, below1, corner, probe, root, jnp.asarray(rights), jnp.asarray(lefts))

    below_grad = g_below.at[:, :, :width].add(passed_along(g_corner, "col", 1))
    from_left = passed_along(g_beside, "col", 1)
    probe_grad, from_above = probe_sum(
        (keep0, keep1), (send0, send1), bits, core, others[0], others[1:], below_grad, from_left
    )
    object_grad = g_own.at[:, :, :width].add(from_left)
    object_grad = object_grad.at[:, :width, :].add(from_above)
    return (object_grad, probe_grad)


def solution(mesh):
    in_specs = (
        P(None, "row", "col"),
        P(),
        P(("row", "col"), None, None),
        P(("row", "col")),
        P(("row", "col")),
        P(("row", "col")),
    )
    out_specs = (P(None, "row", "col"), P())
    return jax.shard_map(shards, mesh=mesh, in_specs=in_specs, out_specs=out_specs, check_vma=False)
```
